32 devices in a mesh: groups: 2 (over y), adapter: 4 (over z), tensor: 2 (over x), sub: 2 (over core).
Axes of the slice: x: 2, y: 2, z: 4, core: 2. Of those that a mesh axis runs over, the one named last changes fastest.
Arguments:
- tokens: bfloat16 [8192, 8192], P(('groups', 'adapter'), 'tensor'), parts along dimension 0, may hold values from -6 to 6
- key_value_weight: bfloat16 [8192, 2048], P('tensor', 'sub'), may hold values from -0.0625 to 0.0625
- adapter_down_table: bfloat16 [4, 2, 64, 8192], P('adapter', 'sub', None, 'tensor'), may hold values from -0.0625 to 0.0625
- adapter_up_table: bfloat16 [4, 2, 64, 1024], P('adapter', 'sub'), may hold values from -0.75 to 0.75
- adapter_per_block: int32 [128, 1], P('groups'), parts along dimension 0, may hold values from 0 to 3; in each aligned block of 16 rows (0 to 15, 16 to 31, ...) at most 4 rows name the same one
- adapter_position: int32 [4], replicated, may hold values from 0 to 3, each once
Outputs:
- kv_out: bfloat16 [8192, 2048], P(('groups', 'adapter', 'tensor'), 'sub'), parts along dimension 0
The draws below stay inside these ranges and needn't reach their ends.
There are 2 independent parts, one for each index of `groups`. The reference program is written for one: setup_inputs(seed, part) draws one part's arguments, and reference() takes and returns one part's arrays. A program takes and returns all parts, laid end to end along the dimension named above; an argument that names none is the same for every part. Nothing has to cross between parts.
Inputs may be any that keep to these rules, and one draw needn't show every extreme that they name: `adapter_per_block`: within the 16 blocks of one index of adapter (aligned runs of 16 rows), no adapter is named by more than 4 blocks. A permutation: adapter a is stored at position adapter_position[a] of adapter_down_table and adapter_up_table.
All inputs are finite; a program needn't handle non-finite values.
Results may differ from the reference program's by a relative error of at most 0.0095.
Values may be sent and summed in bfloat16 or wider, within the bound.
A program may use at most 128 MiB of HBM per device.

```python
import math
import jax
import jax.numpy as jnp
import numpy as np
from jax import lax

MODEL_WIDTH = 8192
ADAPTER_RANK = 64
BLOCK = 64
KEY_VALUE_FEATS = 1024
TOKENS = 4096
NBLK = 64
NB_DEV = 16
ADAPTER_TOTAL = 4
CAP = 4
N_TENSOR = 2


def steps_of(stream_key, dims, shards, smallest, top_value):
    factor_of, own = 1.0, jax.random.fold_in(stream_key, 6)
    for dim, parts in shards:
        draws = jnp.exp(jax.random.uniform(jax.random.fold_in(own, dim), (parts,), jnp.float32, smallest / len(shards), top_value / len(shards)))
        factor_of = factor_of * jnp.repeat(draws, dims[dim] // parts).reshape([-1 if axis == dim else 1 for axis in range(len(dims))])
    return factor_of


def assign_block(own_key, own, number, rows, number_of, top, bound, lean):
    sequence = jax.random.permutation(own_key, number_of)
    heavy_load, usual = portions_of(number_of, rows * top, bound, lean, True), portions_of(number_of, rows * top, bound, lean, False)
    places = jnp.arange(number_of)

    def named(tallies, rotation):
        used = int((tallies > 0).sum())
        fixed = max(1, used // 4)
        shifted = fixed + (places - fixed + rotation * (used - fixed)) % max(1, number_of - fixed)
        return jnp.zeros((number_of,), jnp.int32).at[sequence[jnp.where(places < fixed, places, shifted)]].set(jnp.asarray(tallies, jnp.int32))

    tallies = jnp.where(number % 4 == 0, named(heavy_load, number // 4), named(usual, number - number // 4 - 1))
    mixed = jax.random.permutation(jax.random.fold_in(own, 3), number_of)
    donor, receiver = mixed[0:number_of // 2 * 2:2], mixed[1:number_of // 2 * 2:2]
    slack = jnp.minimum(tallies[donor] - 1, bound - tallies[receiver]) // 2
    slack = jnp.where((donor == sequence[0]) | (receiver == sequence[0]) | (tallies[receiver] == 0), 0, jnp.maximum(slack, 0))
    shifted = jax.random.randint(jax.random.fold_in(own, 4), (number_of // 2,), 0, 1 << 20) % (slack + 1)
    tallies = tallies.at[donor].add(-shifted).at[receiver].add(shifted)
    items = jnp.searchsorted(jnp.cumsum(tallies), jnp.arange(rows * top), side="right").astype(jnp.int32)
    table = items.reshape(top, rows).T
    table = table[jax.random.permutation(jax.random.fold_in(own, 1), rows)]
    rotation = jax.random.randint(jax.random.fold_in(own, 2), (rows, 1), 0, top)
    return jnp.take_along_axis(table, (jnp.arange(top)[None, :] + rotation) % top, axis=1)


def portions_of(number_of, total, most, skew, full):
    loads = [(1 << 20) // math.isqrt(grade ** skew) + 1 for grade in range(1, number_of + 1)]
    largest = most if full else min(most, max(-(-total // number_of), total * loads[0] // sum(loads)))
    least = 1 if total - largest >= number_of - 1 else 0
    counts, surplus = [largest] + [least] * (number_of - 1), total - largest - least * (number_of - 1)
    while surplus > 0:
        candidates = [i for i in range(1, number_of) if counts[i] < largest] or [i for i in range(1, number_of) if counts[i] < most]
        whole, remaining = sum([loads[i] for i in candidates]), surplus
        for i in candidates:
            more = min(most - counts[i], max(1, remaining * loads[i] // whole), surplus)
            counts[i] = counts[i] + more
            surplus = surplus - more
    return np.array(counts)


def noise(rng, extent, width, most, shards=(), dtype=jnp.bfloat16):
    array = jax.random.normal(rng, extent, jnp.float32) * width
    if len(shards) > 0:
        array = steps_of(rng, extent, shards, -0.22, 0.18) * array
    return jnp.clip(array, min=-most, max=most).astype(dtype)


def setup_inputs(seed: int = 0, part: int = 0) -> dict:
    key_of = jax.random.split(jax.random.key(seed), 7)
    own_keys = jax.random.split(jax.random.fold_in(key_of[6], part), 7)
    tokens = noise(own_keys[0], (TOKENS, MODEL_WIDTH), 1.0, 6.0, ((0, 4), (1, 2)))
    key_value_weight = noise(key_of[1], (MODEL_WIDTH, 2 * KEY_VALUE_FEATS), MODEL_WIDTH ** -0.5, 0.0625, ((0, 2), (1, 2)))
    adapter_down_table = noise(key_of[2], (ADAPTER_TOTAL, 2, ADAPTER_RANK, MODEL_WIDTH), MODEL_WIDTH ** -0.5, 0.0625, ((0, 4), (1, 2), (3, 2)))
    adapter_up_table = noise(key_of[3], (ADAPTER_TOTAL, 2, ADAPTER_RANK, KEY_VALUE_FEATS), ADAPTER_RANK ** -0.5, 0.75, ((0, 4), (1, 2)))
    adapter_per_block_keys = jax.random.split(jax.random.fold_in(own_keys[4], 1), NBLK // NB_DEV)
    adapter_per_block_turns = jax.random.permutation(jax.random.fold_in(own_keys[4], 3), NBLK // NB_DEV)
    adapter_per_block = jax.vmap(lambda own, number: assign_block(jax.random.fold_in(own_keys[4], 2), own, number, NB_DEV, ADAPTER_TOTAL, 1, CAP, 2))(adapter_per_block_keys, adapter_per_block_turns).reshape((NBLK, 1))
    adapter_position = jax.random.permutation(key_of[5], ADAPTER_TOTAL).astype(jnp.int32)
    return {"tokens": tokens, "key_value_weight": key_value_weight, "adapter_down_table": adapter_down_table, "adapter_up_table": adapter_up_table, "adapter_per_block": adapter_per_block, "adapter_position": adapter_position}


def reference(tokens, key_value_weight, adapter_down_table, adapter_up_table, adapter_per_block, adapter_position):
    group_width = MODEL_WIDTH // N_TENSOR
    base = jnp.zeros((TOKENS, 2 * KEY_VALUE_FEATS), jnp.float32)
    for group in range(N_TENSOR):
        part = jnp.dot(tokens[:, group * group_width:(group + 1) * group_width],
                       key_value_weight[group * group_width:(group + 1) * group_width, :],
                       preferred_element_type=jnp.float32).astype(jnp.bfloat16)
        base = base + part.astype(jnp.float32)
    block_slots = adapter_position[adapter_per_block[:, 0]].astype(jnp.int32)
    blocked = tokens.reshape(NBLK, BLOCK, MODEL_WIDTH)

    def one_block(pair):
        block_rows, position_index = pair
        down_couple = adapter_down_table[position_index]
        up_couple = adapter_up_table[position_index]
        halves = []
        for half in range(2):
            lowered = jnp.dot(block_rows, down_couple[half].T, preferred_element_type=jnp.float32)
            halves.append(jnp.dot(lowered, up_couple[half].astype(jnp.float32),
                                  precision=lax.Precision.HIGHEST))
        return jnp.concatenate(halves, axis=1)

    correction = lax.map(one_block, (blocked, block_slots)).reshape(TOKENS, 2 * KEY_VALUE_FEATS)
    return (base + correction).astype(jnp.bfloat16)
```

```python
import functools

import jax
import jax.numpy as jnp
from jax import lax
from jax.experimental import pallas as pl
from jax.experimental.pallas import tpu as pltpu
from jax.sharding import PartitionSpec as P

BLOCK = 64
LANES = 128
CHUNKS = 4
MESH = pl.DeviceIdType.MESH
F32 = jnp.float32
BF16 = jnp.bfloat16


def kernel(
    sizes,
    tok_hbm, w_hbm, down_hbm, up_hbm, block_adapter, position,
    out_ref,
    tok, wgt, down, up, part, peer_part, own, low, fold, low_send, low_recv, total,
    tok_sem, w_sem, own_sem,
    xs, xr, ls, lr, zs, zr, ys, yr, us, ur, uys, uyr,
):
    owners, groups, tensors, mt, ct = sizes
    rows, feats = tok.shape
    cols = wgt.shape[1]
    rank = down.shape[1]
    wide = owners * rank
    out_rows = rows // tensors
    out_blocks = out_rows // BLOCK
    half_blocks = out_blocks // 2
    half = out_rows // 2
    n_i, n_k = out_rows // mt, cols // ct
    tiles = n_i * n_k
    fq = feats // (groups * CHUNKS)
    cq = cols // groups
    z = lax.axis_index("adapter")
    g = lax.axis_index("groups")
    t = lax.axis_index("tensor")

    def peer(d):
        return lax.rem(t + d, tensors)

    def group(e):
        return lax.rem(g + e, groups)

    order = list(range(1, tensors)) + [0]

    def tok_load(d, i):
        r = pl.ds(pl.multiple_of(peer(d) * out_rows + i * mt, mt), mt)
        return pltpu.make_async_copy(tok_hbm.at[r, :], tok.at[r, :], tok_sem.at[d, i])

    def w_load(k):
        c = pl.ds(pl.multiple_of(k * ct, ct), ct)
        return pltpu.make_async_copy(w_hbm.at[:, c], wgt.at[:, c], w_sem.at[k])

    def own_loads():
        return (
            pltpu.make_async_copy(down_hbm.at[0, 0], down.at[z], own_sem.at[0]),
            pltpu.make_async_copy(up_hbm.at[0, 0], up.at[z], own_sem.at[1]),
        )

    def feat(h, c):
        return pl.ds(pl.multiple_of((h * CHUNKS + c) * fq, fq), fq)

    def ucol(h):
        return pl.ds(pl.multiple_of(h * cq, cq), cq)

    def zcopy(step, j, c, first=False):
        src = down_hbm.at[0, 0, :, feat(g, c)] if first else down.at[j, :, feat(g, c)]
        return pltpu.make_async_remote_copy(
            src_ref=src, dst_ref=down.at[j, :, feat(g, c)],
            send_sem=zs.at[(step + 1) // 2, j, c], recv_sem=zr.at[j, c],
            device_id={"adapter": z + step}, device_id_type=MESH)

    def ycopy(e, j, h, c):
        return pltpu.make_async_remote_copy(
            src_ref=down.at[j, :, feat(h, c)], dst_ref=down.at[j, :, feat(h, c)],
            send_sem=ys.at[e - 1, j, c], recv_sem=yr.at[j, h, c],
            device_id={"groups": group(e)}, device_id_type=MESH)

    def ucopy(step, j, first=False):
        src = up_hbm.at[0, 0, :, ucol(g)] if first else up.at[j, :, ucol(g)]
        return pltpu.make_async_remote_copy(
            src_ref=src, dst_ref=up.at[j, :, ucol(g)],
            send_sem=us.at[(step + 1) // 2, j], recv_sem=ur.at[j],
            device_id={"adapter": z + step}, device_id_type=MESH)

    def uycopy(e, j, h):
        return pltpu.make_async_remote_copy(
            src_ref=up.at[j, :, ucol(h)], dst_ref=up.at[j, :, ucol(h)],
            send_sem=uys.at[e - 1, j], recv_sem=uyr.at[j, h],
            device_id={"groups": group(e)}, device_id_type=MESH)

    def inside(j):
        return (j >= 0) & (j < owners)

    def down_first():
        for c in range(CHUNKS):
            for step in (-1, 1):
                @pl.when(inside(z + step))
                def _():
                    zcopy(step, z, c, True).start()

    def up_first():
        for step in (-1, 1):
            @pl.when(inside(z + step))
            def _():
                ucopy(step, z, True).start()

    def down_on(s, c):
        for side in (-1, 1):
            j = z + side * s

            @pl.when(inside(j))
            def _():
                zcopy(-side, j, c).wait_recv()

                @pl.when(inside(z - side))
                def _():
                    zcopy(-side, j, c).start()
                for e in range(1, groups):
                    ycopy(e, j, g, c).start()

    def up_on(s):
        for side in (-1, 1):
            j = z + side * s

            @pl.when(inside(j))
            def _():
                ucopy(-side, j).wait_recv()

                @pl.when(inside(z - side))
                def _():
                    ucopy(-side, j).start()
                for e in range(1, groups):
                    uycopy(e, j, g).start()

    def tile_at(i, k):
        return (
            pl.ds(pl.multiple_of(i * mt, mt), mt),
            pl.ds(pl.multiple_of(k * ct, ct), ct),
        )

    def xcopy(d, i, k):
        r, c = tile_at(i, k)
        return pltpu.make_async_remote_copy(
            src_ref=part.at[d - 1, r, c], dst_ref=peer_part.at[d - 1, r, c],
            send_sem=xs.at[d - 1, i, k], recv_sem=xr.at[d - 1, i, k],
            device_id={"tensor": peer(d)}, device_id_type=MESH)

    def lcopy(d):
        return pltpu.make_async_remote_copy(
            src_ref=low_send.at[d - 1], dst_ref=low_recv.at[d - 1],
            send_sem=ls.at[d - 1], recv_sem=lr.at[d - 1],
            device_id={"tensor": peer(d)}, device_id_type=MESH)

    tok_load(order[0], 0).start()
    w_load(0).start()
    for k in range(1, n_k):
        w_load(k).start()
    for n, d in enumerate(order):
        for i in range(n_i):
            if n or i:
                tok_load(d, i).start()
    for copy in own_loads():
        copy.start()

    barrier = pltpu.get_barrier_semaphore()
    for step in (-1, 1):
        @pl.when(inside(z + step))
        def _():
            pl.semaphore_signal(barrier, inc=1, device_id={"adapter": z + step}, device_id_type=MESH)
    for e in range(1, groups):
        pl.semaphore_signal(barrier, inc=1, device_id={"groups": group(e)}, device_id_type=MESH)
    for d in range(1, tensors):
        pl.semaphore_signal(barrier, inc=1, device_id={"tensor": peer(d)}, device_id_type=MESH)
    ends = jnp.where(z == 0, 1, 0) + jnp.where(z == owners - 1, 1, 0)
    pl.semaphore_wait(barrier, groups + tensors - ends)
    down_first()

    for n, d in enumerate(order):
        def tile(step, carry, n=n, d=d):
            i, k = step // n_k, step % n_k

            @pl.when(k == 0)
            def _():
                tok_load(d, i).wait()
            if n == 0:
                @pl.when(i == 0)
                def _():
                    w_load(k).wait()
            r, c = tile_at(i, k)
            tr = pl.ds(pl.multiple_of(peer(d) * out_rows + i * mt, mt), mt)
            value = jnp.dot(tok[tr, :], wgt[:, c], preferred_element_type=F32)
            if d:
                part[d - 1, r, c] = value.astype(BF16)
                xcopy(d, i, k).start()
            else:
                own[r, c] = value
            s = 1 if n == tensors - 2 else 2 if n == tensors - 1 else 0
            if 0 < s < owners - 1:
                @pl.when(step >= tiles - CHUNKS)
                def _():
                    down_on(s, step - (tiles - CHUNKS))
            return carry

        lax.fori_loop(0, tiles, tile, 0)
        if n == tensors - 2:
            up_first()
    for copy in own_loads():
        copy.wait()
    if owners > 2:
        up_on(1)
    for s in range(3, owners - 1):
        for c in range(CHUNKS):
            down_on(s, c)
        up_on(s - 1)

    def lower(r, h, c, first=False):
        f = feat(h, c)
        table = down[:, :, f].reshape(wide, fq)
        value = lax.dot_general(
            tok[r, f], table, (((1,), (1,)), ((), ())), preferred_element_type=F32)
        if first:
            low[r, :] = value
        else:
            low[r, :] = low[r, :] + value

    def across(e, c):
        h = group(e)

        def one(j, carry):
            @pl.when(j != z)
            def _():
                ycopy(e, j, h, c).wait_recv()
            return carry

        lax.fori_loop(0, owners, one, 0)

    everything = pl.ds(0, rows)
    jobs = []
    for c in range(CHUNKS):
        jobs.append((0, c))
        if c:
            jobs += [(e, c - 1) for e in range(1, groups)]
    jobs += [(e, CHUNKS - 1) for e in range(1, groups)]
    for n, (e, c) in enumerate(jobs):
        if e == 0:
            if owners > 1:
                down_on(owners - 1, c)
        else:
            across(e, c)
        if n < len(jobs) - 1:
            lower(everything, group(e), c, n == 0)
    if owners > 3:
        up_on(owners - 2)

    lane = lax.broadcasted_iota(jnp.int32, (BLOCK, LANES), 1)
    wide_lane = lax.broadcasted_iota(jnp.int32, (BLOCK, wide), 1) // rank

    def slot(d, b):
        at = z * (rows // BLOCK) + peer(d) * out_blocks + b
        return position[block_adapter[at]]

    def folded(d, b):
        r = pl.ds(pl.multiple_of(peer(d) * out_rows + b * BLOCK, BLOCK), BLOCK)
        kept = jnp.where(wide_lane == slot(d, b), low[r, :], 0.0)
        value = kept[:, :LANES]
        for n in range(1, wide // LANES):
            value = value + kept[:, n * LANES:(n + 1) * LANES]
        return value + pltpu.roll(value, rank, 1)

    e, c = jobs[-1]
    for d in order:
        r = pl.ds(pl.multiple_of(peer(d) * out_rows, out_rows), out_rows)
        lower(r, group(e), c)
        if d:
            for b in range(half_blocks):
                low_send[d - 1, b * BLOCK:(b + 1) * BLOCK, :] = jnp.where(
                    lane < rank, folded(d, b), folded(d, b + half_blocks)).astype(BF16)
            lcopy(d).start()
        else:
            for b in range(out_blocks):
                fold[b * BLOCK:(b + 1) * BLOCK, :] = folded(d, b)

    if owners > 1:
        up_on(owners - 1)
    for e in range(1, groups):
        def one(j, carry, e=e):
            @pl.when(j != z)
            def _():
                uycopy(e, j, group(e)).wait_recv()
            return carry

        lax.fori_loop(0, owners, one, 0)

    for d in range(1, tensors):
        lcopy(d).wait_recv()
    for b in range(half_blocks):
        at = pl.ds(b * BLOCK, BLOCK)
        first, second = fold[at, :], fold[pl.ds((b + half_blocks) * BLOCK, BLOCK), :]
        for d in range(1, tensors):
            got = low_recv[d - 1, at, :].astype(F32)
            other = pltpu.roll(got, rank, 1)
            first = first + jnp.where(lane < rank, got, other)
            second = second + jnp.where(lane < rank, other, got)
        for value, block in ((first, b), (second, b + half_blocks)):
            spread = jnp.concatenate([value] * (wide // LANES), axis=1)
            total[block * BLOCK:(block + 1) * BLOCK, :] = jnp.where(
                wide_lane == slot(0, block), spread, 0.0).astype(BF16)

    def finish(step, carry):
        i, k = step // n_k, step % n_k
        r, c = tile_at(i, k)
        value = own[r, c] + jnp.dot(
            total[r, :], up[:, :, c].reshape(wide, ct), preferred_element_type=F32)
        for d in range(1, tensors):
            xcopy(d, i, k).wait_recv()
            value = value + peer_part[d - 1, r, c].astype(F32)
        out_ref[r, c] = value.astype(BF16)
        return carry

    lax.fori_loop(0, tiles, finish, 0)

    for d in range(1, tensors):
        def left(step, carry, d=d):
            xcopy(d, step // n_k, step % n_k).wait_send()
            return carry

        lax.fori_loop(0, tiles, left, 0)
        lcopy(d).wait_send()

    def sent(j, carry):
        for step in (-1, 1):
            @pl.when(inside(z + step) & (step * (z - j) >= 0))
            def _():
                for c in range(CHUNKS):
                    zcopy(step, j, c).wait_send()
                ucopy(step, j).wait_send()

        @pl.when(j != z)
        def _():
            for e in range(1, groups):
                for c in range(CHUNKS):
                    ycopy(e, j, g, c).wait_send()
                uycopy(e, j, g).wait_send()
        return carry

    lax.fori_loop(0, owners, sent, 0)


def shards(mesh, tokens, weight, down, up, block_adapter, position):
    rows, feats = tokens.shape
    cols = weight.shape[1]
    rank = down.shape[2]
    owners, groups, tensors = (mesh.shape[a] for a in ("adapter", "groups", "tensor"))
    out_rows = rows // tensors
    mt, ct = min(256, out_rows), 256
    n_i, n_k = out_rows // mt, cols // ct
    wide = owners * rank
    peers, others = max(tensors - 1, 1), max(groups - 1, 1)
    dma = pltpu.SemaphoreType.DMA
    hbm = pl.BlockSpec(memory_space=pl.ANY)
    smem = pl.BlockSpec(memory_space=pltpu.SMEM)
    flops = 2 * rows * feats * (cols + wide) + 2 * out_rows * wide * cols
    return pl.pallas_call(
        functools.partial(kernel, (owners, groups, tensors, mt, ct)),
        out_shape=jax.ShapeDtypeStruct((out_rows, cols), BF16),
        in_specs=[hbm, hbm, hbm, hbm, smem, smem],
        out_specs=pl.BlockSpec(memory_space=pltpu.VMEM),
        scratch_shapes=[
            pltpu.VMEM((rows, feats), BF16),
            pltpu.VMEM((feats, cols), BF16),
            pltpu.VMEM((owners, rank, feats), BF16),
            pltpu.VMEM((owners, rank, cols), BF16),
            pltpu.VMEM((peers, out_rows, cols), BF16),
            pltpu.VMEM((peers, out_rows, cols), BF16),
            pltpu.VMEM((out_rows, cols), F32),
            pltpu.VMEM((rows, wide), F32),
            pltpu.VMEM((out_rows, LANES), F32),
            pltpu.VMEM((peers, out_rows // 2, LANES), BF16),
            pltpu.VMEM((peers, out_rows // 2, LANES), BF16),
            pltpu.VMEM((out_rows, wide), BF16),
            dma((tensors, n_i)),
            dma((n_k,)),
            dma((2,)),
            dma((peers, n_i, n_k)),
            dma((peers, n_i, n_k)),
            dma((peers,)),
            dma((peers,)),
            dma((2, owners, CHUNKS)),
            dma((owners, CHUNKS)),
            dma((others, owners, CHUNKS)),
            dma((owners, groups, CHUNKS)),
            dma((2, owners)),
            dma((owners,)),
            dma((others, owners)),
            dma((owners, groups)),
        ],
        compiler_params=pltpu.CompilerParams(
            collective_id=0, has_side_effects=True, vmem_limit_bytes=56 * 2**20),
        cost_estimate=pl.CostEstimate(
            flops=flops, bytes_accessed=2 * (rows * feats + feats * cols), transcendentals=0),
    )(tokens, weight, down, up, block_adapter.reshape(-1), position)


def solution(mesh):
    placed = (
        P(("groups", "adapter"), "tensor"),
        P("tensor", "sub"),
        P("adapter", "sub", None, "tensor"),
        P("adapter", "sub", None, None),
        P("groups", None),
        P(),
    )
    return jax.shard_map(
        functools.partial(shards, mesh),
        mesh=mesh,
        in_specs=placed,
        out_specs=P(("groups", "adapter", "tensor"), "sub"),
        check_vma=False,
    )
```

```python
import functools

import jax
import jax.numpy as jnp
from jax import lax
from jax.experimental import pallas as pl
from jax.experimental.pallas import tpu as pltpu
from jax.sharding import PartitionSpec as P

BLOCK = 64
LANES = 128
CHUNKS = 4
MESH = pl.DeviceIdType.MESH
F32 = jnp.float32
BF16 = jnp.bfloat16


def kernel(
    sizes,
    tok_hbm, w_hbm, down_hbm, up_hbm, block_adapter, position,
    out_ref,
    tok, wgt, down, up, part, peer_part, own, low, fold, low_send, low_recv, total,
    tok_sem, w_sem, own_sem,
    xs, xr, ls, lr, zs, zr, ys, yr, us, ur, uys, uyr,
):
    owners, groups, tensors, mt, ct = sizes
    rows, feats = tok.shape
    cols = wgt.shape[1]
    rank = down.shape[1]
    wide = owners * rank
    out_rows = rows // tensors
    out_blocks = out_rows // BLOCK
    half_blocks = out_blocks // 2
    half = out_rows // 2
    n_i, n_k = out_rows // mt, cols // ct
    tiles = n_i * n_k
    fq = feats // (groups * CHUNKS)
    cq = cols // groups
    z = lax.axis_index("adapter")
    g = lax.axis_index("groups")
    t = lax.axis_index("tensor")

    def peer(d):
        return lax.rem(t + d, tensors)

    def group(e):
        return lax.rem(g + e, groups)

    order = list(range(1, tensors)) + [0]

    def tok_load(d, i):
        r = pl.ds(pl.multiple_of(peer(d) * out_rows + i * mt, mt), mt)
        return pltpu.make_async_copy(tok_hbm.at[r, :], tok.at[r, :], tok_sem.at[d, i])

    def w_load(k):
        c = pl.ds(pl.multiple_of(k * ct, ct), ct)
        return pltpu.make_async_copy(w_hbm.at[:, c], wgt.at[:, c], w_sem.at[k])

    def own_loads():
        return (
            pltpu.make_async_copy(down_hbm.at[0, 0], down.at[z], own_sem.at[0]),
            pltpu.make_async_copy(up_hbm.at[0, 0], up.at[z], own_sem.at[1]),
        )

    def feat(h, c):
        return pl.ds(pl.multiple_of((h * CHUNKS + c) * fq, fq), fq)

    def ucol(h):
        return pl.ds(pl.multiple_of(h * cq, cq), cq)

    def zcopy(step, j, c, first=False):
        src = down_hbm.at[0, 0, :, feat(g, c)] if first else down.at[j, :, feat(g, c)]
        return pltpu.make_async_remote_copy(
            src_ref=src, dst_ref=down.at[j, :, feat(g, c)],
            send_sem=zs.at[(step + 1) // 2, j, c], recv_sem=zr.at[j, c],
            device_id={"adapter": z + step}, device_id_type=MESH)

    def ycopy(e, j, h, c):
        return pltpu.make_async_remote_copy(
            src_ref=down.at[j, :, feat(h, c)], dst_ref=down.at[j, :, feat(h, c)],
            send_sem=ys.at[e - 1, j, c], recv_sem=yr.at[j, h, c],
            device_id={"groups": group(e)}, device_id_type=MESH)

    def ucopy(step, j, first=False):
        src = up_hbm.at[0, 0, :, ucol(g)] if first else up.at[j, :, ucol(g)]
        return pltpu.make_async_remote_copy(
            src_ref=src, dst_ref=up.at[j, :, ucol(g)],
            send_sem=us.at[(step + 1) // 2, j], recv_sem=ur.at[j],
            device_id={"adapter": z + step}, device_id_type=MESH)

    def uycopy(e, j, h):
        return pltpu.make_async_remote_copy(
            src_ref=up.at[j, :, ucol(h)], dst_ref=up.at[j, :, ucol(h)],
            send_sem=uys.at[e - 1, j], recv_sem=uyr.at[j, h],
            device_id={"groups": group(e)}, device_id_type=MESH)

    def inside(j):
        return (j >= 0) & (j < owners)

    def down_first():
        for c in range(CHUNKS):
            for step in (-1, 1):
                @pl.when(inside(z + step))
                def _():
                    zcopy(step, z, c, True).start()

    def up_first():
        for step in (-1, 1):
            @pl.when(inside(z + step))
            def _():
                ucopy(step, z, True).start()

    def down_on(s, c):
        for side in (-1, 1):
            j = z + side * s

            @pl.when(inside(j))
            def _():
                zcopy(-side, j, c).wait_recv()

                @pl.when(inside(z - side))
                def _():
                    zcopy(-side, j, c).start()
                for e in range(1, groups):
                    ycopy(e, j, g, c).start()

    def up_on(s):
        for side in (-1, 1):
            j = z + side * s

            @pl.when(inside(j))
            def _():
                ucopy(-side, j).wait_recv()

                @pl.when(inside(z - side))
                def _():
                    ucopy(-side, j).start()
                for e in range(1, groups):
                    uycopy(e, j, g).start()

    def tile_at(i, k):
        return (
            pl.ds(pl.multiple_of(i * mt, mt), mt),
            pl.ds(pl.multiple_of(k * ct, ct), ct),
        )

    def xcopy(d, i, k):
        r, c = tile_at(i, k)
        return pltpu.make_async_remote_copy(
            src_ref=part.at[d - 1, r, c], dst_ref=peer_part.at[d - 1, r, c],
            send_sem=xs.at[d - 1, i, k], recv_sem=xr.at[d - 1, i, k],
            device_id={"tensor": peer(d)}, device_id_type=MESH)

    def lcopy(d):
        return pltpu.make_async_remote_copy(
            src_ref=low_send.at[d - 1], dst_ref=low_recv.at[d - 1],
            send_sem=ls.at[d - 1], recv_sem=lr.at[d - 1],
            device_id={"tensor": peer(d)}, device_id_type=MESH)

    queue = [functools.partial(w_load, k) for k in range(1, n_k)]
    queue += [
        functools.partial(tok_load, d, i)
        for n, d in enumerate(order) for i in range(n_i) if n or i
    ]
    tok_load(order[0], 0).start()
    w_load(0).start()
    queue[0]().start()
    ahead = n_k - 1
    groups_of_loads = [queue[1:2]] + [queue[n:n + 1] for n in range(2, ahead + 1)]
    groups_of_loads.append(queue[ahead + 1:])

    barrier = pltpu.get_barrier_semaphore()
    for step in (-1, 1):
        @pl.when(inside(z + step))
        def _():
            pl.semaphore_signal(barrier, inc=1, device_id={"adapter": z + step}, device_id_type=MESH)
    for e in range(1, groups):
        pl.semaphore_signal(barrier, inc=1, device_id={"groups": group(e)}, device_id_type=MESH)
    for d in range(1, tensors):
        pl.semaphore_signal(barrier, inc=1, device_id={"tensor": peer(d)}, device_id_type=MESH)
    ends = jnp.where(z == 0, 1, 0) + jnp.where(z == owners - 1, 1, 0)
    pl.semaphore_wait(barrier, groups + tensors - ends)
    down_first()

    for n, d in enumerate(order):
        def tile(step, carry, n=n, d=d):
            i, k = step // n_k, step % n_k

            @pl.when(k == 0)
            def _():
                tok_load(d, i).wait()
            if n == 0:
                @pl.when(i == 0)
                def _():
                    w_load(k).wait()
            if n == 0:
                for at, loads in enumerate(groups_of_loads):
                    @pl.when(step == at)
                    def _(loads=loads, at=at):
                        for load in loads:
                            load().start()
                        if at == len(groups_of_loads) - 1:
                            for copy in own_loads():
                                copy.start()
            r, c = tile_at(i, k)
            tr = pl.ds(pl.multiple_of(peer(d) * out_rows + i * mt, mt), mt)
            value = jnp.dot(tok[tr, :], wgt[:, c], preferred_element_type=F32)
            if d:
                part[d - 1, r, c] = value.astype(BF16)
                xcopy(d, i, k).start()
            else:
                own[r, c] = value
            if owners > 2:
                if n == tensors - 2:
                    @pl.when(step >= tiles - CHUNKS)
                    def _():
                        down_on(1, step - (tiles - CHUNKS))
                if n == tensors - 1 and owners > 3:
                    @pl.when(step >= tiles - CHUNKS)
                    def _():
                        down_on(2, step - (tiles - CHUNKS))
            return carry

        lax.fori_loop(0, tiles, tile, 0)
        if n == tensors - 2:
            up_first()
    for copy in own_loads():
        copy.wait()
    if owners > 3:
        up_on(1)
    for s in range(3, owners - 1):
        for c in range(CHUNKS):
            down_on(s, c)
        up_on(s - 1)

    def lower(r, h, c, first=False):
        f = feat(h, c)
        table = down[:, :, f].reshape(wide, fq)
        value = lax.dot_general(
            tok[r, f], table, (((1,), (1,)), ((), ())), preferred_element_type=F32)
        if first:
            low[r, :] = value
        else:
            low[r, :] = low[r, :] + value

    def across(e, c):
        h = group(e)

        def one(j, carry):
            @pl.when(j != z)
            def _():
                ycopy(e, j, h, c).wait_recv()
            return carry

        lax.fori_loop(0, owners, one, 0)

    everything = pl.ds(0, rows)
    jobs = [(e, c) for e in range(groups) for c in range(CHUNKS)]
    for n, (e, c) in enumerate(jobs):
        if e == 0:
            if owners > 1:
                down_on(owners - 1, c)
        else:
            across(e, c)
        if n < len(jobs) - 1:
            lower(everything, group(e), c, n == 0)
        if n == CHUNKS - 1 and owners > 2:
            up_on(owners - 2)

    lane = lax.broadcasted_iota(jnp.int32, (BLOCK, LANES), 1)
    wide_lane = lax.broadcasted_iota(jnp.int32, (BLOCK, wide), 1) // rank

    def slot(d, b):
        at = z * (rows // BLOCK) + peer(d) * out_blocks + b
        return position[block_adapter[at]]

    def folded(d, b):
        r = pl.ds(pl.multiple_of(peer(d) * out_rows + b * BLOCK, BLOCK), BLOCK)
        kept = jnp.where(wide_lane == slot(d, b), low[r, :], 0.0)
        value = kept[:, :LANES]
        for n in range(1, wide // LANES):
            value = value + kept[:, n * LANES:(n + 1) * LANES]
        return value + pltpu.roll(value, rank, 1)

    e, c = jobs[-1]
    for d in order:
        r = pl.ds(pl.multiple_of(peer(d) * out_rows, out_rows), out_rows)
        lower(r, group(e), c)
        if d:
            for b in range(half_blocks):
                low_send[d - 1, b * BLOCK:(b + 1) * BLOCK, :] = jnp.where(
                    lane < rank, folded(d, b), folded(d, b + half_blocks)).astype(BF16)
            lcopy(d).start()
        else:
            for b in range(out_blocks):
                fold[b * BLOCK:(b + 1) * BLOCK, :] = folded(d, b)

    if owners > 1:
        up_on(owners - 1)
    for e in range(1, groups):
        def one(j, carry, e=e):
            @pl.when(j != z)
            def _():
                uycopy(e, j, group(e)).wait_recv()
            return carry

        lax.fori_loop(0, owners, one, 0)

    def gather(step, carry):
        i, k = step // n_k, step % n_k
        r, c = tile_at(i, k)
        value = own[r, c]
        for d in range(1, tensors):
            xcopy(d, i, k).wait_recv()
            value = value + peer_part[d - 1, r, c].astype(F32)
        own[r, c] = value
        return carry

    lax.fori_loop(0, tiles, gather, 0)
    for d in range(1, tensors):
        lcopy(d).wait_recv()
    for b in range(half_blocks):
        at = pl.ds(b * BLOCK, BLOCK)
        first, second = fold[at, :], fold[pl.ds((b + half_blocks) * BLOCK, BLOCK), :]
        for d in range(1, tensors):
            got = low_recv[d - 1, at, :].astype(F32)
            other = pltpu.roll(got, rank, 1)
            first = first + jnp.where(lane < rank, got, other)
            second = second + jnp.where(lane < rank, other, got)
        for value, block in ((first, b), (second, b + half_blocks)):
            spread = jnp.concatenate([value] * (wide // LANES), axis=1)
            total[block * BLOCK:(block + 1) * BLOCK, :] = jnp.where(
                wide_lane == slot(0, block), spread, 0.0).astype(BF16)

    def finish(step, carry):
        i, k = step // n_k, step % n_k
        r, c = tile_at(i, k)
        value = own[r, c] + jnp.dot(
            total[r, :], up[:, :, c].reshape(wide, ct), preferred_element_type=F32)
        out_ref[r, c] = value.astype(BF16)
        return carry

    lax.fori_loop(0, tiles, finish, 0)

    for d in range(1, tensors):
        def left(step, carry, d=d):
            xcopy(d, step // n_k, step % n_k).wait_send()
            return carry

        lax.fori_loop(0, tiles, left, 0)
        lcopy(d).wait_send()

    def sent(j, carry):
        for step in (-1, 1):
            @pl.when(inside(z + step) & (step * (z - j) >= 0))
            def _():
                for c in range(CHUNKS):
                    zcopy(step, j, c).wait_send()
                ucopy(step, j).wait_send()

        @pl.when(j != z)
        def _():
            for e in range(1, groups):
                for c in range(CHUNKS):
                    ycopy(e, j, g, c).wait_send()
                uycopy(e, j, g).wait_send()
        return carry

    lax.fori_loop(0, owners, sent, 0)


def shards(mesh, tokens, weight, down, up, block_adapter, position):
    rows, feats = tokens.shape
    cols = weight.shape[1]
    rank = down.shape[2]
    owners, groups, tensors = (mesh.shape[a] for a in ("adapter", "groups", "tensor"))
    out_rows = rows // tensors
    mt, ct = min(256, out_rows), 256
    n_i, n_k = out_rows // mt, cols // ct
    wide = owners * rank
    peers, others = max(tensors - 1, 1), max(groups - 1, 1)
    dma = pltpu.SemaphoreType.DMA
    hbm = pl.BlockSpec(memory_space=pl.ANY)
    smem = pl.BlockSpec(memory_space=pltpu.SMEM)
    flops = 2 * rows * feats * (cols + wide) + 2 * out_rows * wide * cols
    return pl.pallas_call(
        functools.partial(kernel, (owners, groups, tensors, mt, ct)),
        out_shape=pltpu.VMEM((out_rows, cols), BF16),
        in_specs=[hbm, hbm, hbm, hbm, smem, smem],
        out_specs=pl.BlockSpec(memory_space=pltpu.VMEM),
        scratch_shapes=[
            pltpu.VMEM((rows, feats), BF16),
            pltpu.VMEM((feats, cols), BF16),
            pltpu.VMEM((owners, rank, feats), BF16),
            pltpu.VMEM((owners, rank, cols), BF16),
            pltpu.VMEM((peers, out_rows, cols), BF16),
            pltpu.VMEM((peers, out_rows, cols), BF16),
            pltpu.VMEM((out_rows, cols), F32),
            pltpu.VMEM((rows, wide), F32),
            pltpu.VMEM((out_rows, LANES), F32),
            pltpu.VMEM((peers, out_rows // 2, LANES), BF16),
            pltpu.VMEM((peers, out_rows // 2, LANES), BF16),
            pltpu.VMEM((out_rows, wide), BF16),
            dma((tensors, n_i)),
            dma((n_k,)),
            dma((2,)),
            dma((peers, n_i, n_k)),
            dma((peers, n_i, n_k)),
            dma((peers,)),
            dma((peers,)),
            dma((2, owners, CHUNKS)),
            dma((owners, CHUNKS)),
            dma((others, owners, CHUNKS)),
            dma((owners, groups, CHUNKS)),
            dma((2, owners)),
            dma((owners,)),
            dma((others, owners)),
            dma((owners, groups)),
        ],
        compiler_params=pltpu.CompilerParams(
            collective_id=0, has_side_effects=True, vmem_limit_bytes=56 * 2**20),
        cost_estimate=pl.CostEstimate(
            flops=flops, bytes_accessed=2 * (rows * feats + feats * cols), transcendentals=0),
    )(tokens, weight, down, up, block_adapter.reshape(-1), position)


def solution(mesh):
    placed = (
        P(("groups", "adapter"), "tensor"),
        P("tensor", "sub"),
        P("adapter", "sub", None, "tensor"),
        P("adapter", "sub", None, None),
        P("groups", None),
        P(),
    )
    return jax.shard_map(
        functools.partial(shards, mesh),
        mesh=mesh,
        in_specs=placed,
        out_specs=P(("groups", "adapter", "tensor"), "sub"),
        check_vma=False,
    )
```

```python
import functools

import jax
import jax.numpy as jnp
from jax import lax
from jax.experimental import pallas as pl
from jax.experimental.pallas import tpu as pltpu
from jax.sharding import PartitionSpec as P

BLOCK = 64
LANES = 128
CHUNKS = 4
MESH = pl.DeviceIdType.MESH
F32 = jnp.float32
BF16 = jnp.bfloat16


def kernel(
    sizes,
    tok_hbm, w_hbm, down_hbm, up_hbm, block_adapter, position,
    out_ref,
    tok, wgt, down, up, part, peer_part, own, low, fold, low_send, low_recv, total,
    tok_sem, w_sem, own_sem,
    xs, xr, ls, lr, zs, zr, ys, yr, us, ur, uys, uyr,
):
    owners, groups, tensors, mt, ct = sizes
    rows, feats = tok.shape
    cols = wgt.shape[1]
    rank = down.shape[1]
    wide = owners * rank
    out_rows = rows // tensors
    out_blocks = out_rows // BLOCK
    half_blocks = out_blocks // 2
    half = out_rows // 2
    n_i, n_k = out_rows // mt, cols // ct
    tiles = n_i * n_k
    fq = feats // (groups * CHUNKS)
    cq = cols // groups
    z = lax.axis_index("adapter")
    g = lax.axis_index("groups")
    t = lax.axis_index("tensor")

    def peer(d):
        return lax.rem(t + d, tensors)

    def group(e):
        return lax.rem(g + e, groups)

    order = list(range(1, tensors)) + [0]

    def tok_load(d, i):
        r = pl.ds(pl.multiple_of(peer(d) * out_rows + i * mt, mt), mt)
        return pltpu.make_async_copy(tok_hbm.at[r, :], tok.at[r, :], tok_sem.at[d, i])

    def w_load(k):
        c = pl.ds(pl.multiple_of(k * ct, ct), ct)
        return pltpu.make_async_copy(w_hbm.at[:, c], wgt.at[:, c], w_sem.at[k])

    def own_loads():
        return (
            pltpu.make_async_copy(down_hbm.at[0, 0], down.at[z], own_sem.at[0]),
            pltpu.make_async_copy(up_hbm.at[0, 0], up.at[z], own_sem.at[1]),
        )

    def feat(h, c):
        return pl.ds(pl.multiple_of((h * CHUNKS + c) * fq, fq), fq)

    def ucol(h):
        return pl.ds(pl.multiple_of(h * cq, cq), cq)

    def zcopy(step, j, c, first=False):
        src = down_hbm.at[0, 0, :, feat(g, c)] if first else down.at[j, :, feat(g, c)]
        return pltpu.make_async_remote_copy(
            src_ref=src, dst_ref=down.at[j, :, feat(g, c)],
            send_sem=zs.at[(step + 1) // 2, j, c], recv_sem=zr.at[j, c],
            device_id={"adapter": z + step}, device_id_type=MESH)

    def ycopy(e, j, h, c):
        return pltpu.make_async_remote_copy(
            src_ref=down.at[j, :, feat(h, c)], dst_ref=down.at[j, :, feat(h, c)],
            send_sem=ys.at[e - 1, j, c], recv_sem=yr.at[j, h, c],
            device_id={"groups": group(e)}, device_id_type=MESH)

    def ucopy(step, j, first=False):
        src = up_hbm.at[0, 0, :, ucol(g)] if first else up.at[j, :, ucol(g)]
        return pltpu.make_async_remote_copy(
            src_ref=src, dst_ref=up.at[j, :, ucol(g)],
            send_sem=us.at[(step + 1) // 2, j], recv_sem=ur.at[j],
            device_id={"adapter": z + step}, device_id_type=MESH)

    def uycopy(e, j, h):
        return pltpu.make_async_remote_copy(
            src_ref=up.at[j, :, ucol(h)], dst_ref=up.at[j, :, ucol(h)],
            send_sem=uys.at[e - 1, j], recv_sem=uyr.at[j, h],
            device_id={"groups": group(e)}, device_id_type=MESH)

    def inside(j):
        return (j >= 0) & (j < owners)

    def down_first():
        for c in range(CHUNKS):
            for step in (-1, 1):
                @pl.when(inside(z + step))
                def _():
                    zcopy(step, z, c, True).start()

    def up_first():
        for step in (-1, 1):
            @pl.when(inside(z + step))
            def _():
                ucopy(step, z, True).start()

    def down_on(s, c):
        for side in (-1, 1):
            j = z + side * s

            @pl.when(inside(j))
            def _():
                zcopy(-side, j, c).wait_recv()

                @pl.when(inside(z - side))
                def _():
                    zcopy(-side, j, c).start()
                for e in range(1, groups):
                    ycopy(e, j, g, c).start()

    def up_on(s):
        for side in (-1, 1):
            j = z + side * s

            @pl.when(inside(j))
            def _():
                ucopy(-side, j).wait_recv()

                @pl.when(inside(z - side))
                def _():
                    ucopy(-side, j).start()
                for e in range(1, groups):
                    uycopy(e, j, g).start()

    def tile_at(i, k):
        return (
            pl.ds(pl.multiple_of(i * mt, mt), mt),
            pl.ds(pl.multiple_of(k * ct, ct), ct),
        )

    def xcopy(d, i, k):
        r, c = tile_at(i, k)
        return pltpu.make_async_remote_copy(
            src_ref=part.at[d - 1, r, c], dst_ref=peer_part.at[d - 1, r, c],
            send_sem=xs.at[d - 1, i, k], recv_sem=xr.at[d - 1, i, k],
            device_id={"tensor": peer(d)}, device_id_type=MESH)

    def lcopy(d):
        return pltpu.make_async_remote_copy(
            src_ref=low_send.at[d - 1], dst_ref=low_recv.at[d - 1],
            send_sem=ls.at[d - 1], recv_sem=lr.at[d - 1],
            device_id={"tensor": peer(d)}, device_id_type=MESH)

    queue = [functools.partial(w_load, k) for k in range(1, n_k)]
    queue += [
        functools.partial(tok_load, d, i)
        for n, d in enumerate(order) for i in range(n_i) if n or i
    ]
    tok_load(order[0], 0).start()
    w_load(0).start()
    ahead = n_k - 1
    groups_of_loads = [queue[0:2]] + [queue[n:n + 1] for n in range(2, ahead + 1)]
    groups_of_loads.append(queue[ahead + 1:])

    barrier = pltpu.get_barrier_semaphore()
    for step in (-1, 1):
        @pl.when(inside(z + step))
        def _():
            pl.semaphore_signal(barrier, inc=1, device_id={"adapter": z + step}, device_id_type=MESH)
    for e in range(1, groups):
        pl.semaphore_signal(barrier, inc=1, device_id={"groups": group(e)}, device_id_type=MESH)
    for d in range(1, tensors):
        pl.semaphore_signal(barrier, inc=1, device_id={"tensor": peer(d)}, device_id_type=MESH)
    ends = jnp.where(z == 0, 1, 0) + jnp.where(z == owners - 1, 1, 0)
    pl.semaphore_wait(barrier, groups + tensors - ends)
    down_first()

    early = (tiles - CHUNKS) // 2
    for n, d in enumerate(order):
        def tile(step, carry, n=n, d=d):
            i, k = step // n_k, step % n_k

            @pl.when(k == 0)
            def _():
                tok_load(d, i).wait()
            if n == 0:
                @pl.when(i == 0)
                def _():
                    w_load(k).wait()
            if n == 0:
                for at, loads in enumerate(groups_of_loads):
                    @pl.when(step == at)
                    def _(loads=loads, at=at):
                        for load in loads:
                            load().start()
                        if at == len(groups_of_loads) - 1:
                            for copy in own_loads():
                                copy.start()
            r, c = tile_at(i, k)
            tr = pl.ds(pl.multiple_of(peer(d) * out_rows + i * mt, mt), mt)
            value = jnp.dot(tok[tr, :], wgt[:, c], preferred_element_type=F32)
            if d:
                part[d - 1, r, c] = value.astype(BF16)
                xcopy(d, i, k).start()
            else:
                own[r, c] = value
            if owners > 2:
                if n == tensors - 2:
                    @pl.when((step >= early) & (step < early + CHUNKS))
                    def _():
                        down_on(1, step - early)
                if n == tensors - 1 and owners > 3:
                    @pl.when((step >= early) & (step < early + CHUNKS))
                    def _():
                        down_on(2, step - early)
            return carry

        lax.fori_loop(0, tiles, tile, 0)
        if n == tensors - 2:
            up_first()
    for copy in own_loads():
        copy.wait()
    if owners > 3:
        up_on(1)
    for s in range(3, owners - 1):
        for c in range(CHUNKS):
            down_on(s, c)
        up_on(s - 1)

    def lower(r, h, c, first=False):
        f = feat(h, c)
        table = down[:, :, f].reshape(wide, fq)
        value = lax.dot_general(
            tok[r, f], table, (((1,), (1,)), ((), ())), preferred_element_type=F32)
        if first:
            low[r, :] = value
        else:
            low[r, :] = low[r, :] + value

    def across(e, c):
        h = group(e)

        def one(j, carry):
            @pl.when(j != z)
            def _():
                ycopy(e, j, h, c).wait_recv()
            return carry

        lax.fori_loop(0, owners, one, 0)

    everything = pl.ds(0, rows)
    jobs = [(e, c) for e in range(groups) for c in range(CHUNKS)]
    for n, (e, c) in enumerate(jobs):
        if e == 0:
            if owners > 1:
                down_on(owners - 1, c)
        else:
            across(e, c)
        if n < len(jobs) - 1:
            lower(everything, group(e), c, n == 0)
        if n == CHUNKS - 1 and owners > 2:
            up_on(owners - 2)
        if n == len(jobs) - 2 and owners > 1:
            up_on(owners - 1)

    lane = lax.broadcasted_iota(jnp.int32, (BLOCK, LANES), 1)
    wide_lane = lax.broadcasted_iota(jnp.int32, (BLOCK, wide), 1) // rank

    def slot(d, b):
        at = z * (rows // BLOCK) + peer(d) * out_blocks + b
        return position[block_adapter[at]]

    def folded(d, b):
        r = pl.ds(pl.multiple_of(peer(d) * out_rows + b * BLOCK, BLOCK), BLOCK)
        kept = jnp.where(wide_lane == slot(d, b), low[r, :], 0.0)
        value = kept[:, :LANES]
        for n in range(1, wide // LANES):
            value = value + kept[:, n * LANES:(n + 1) * LANES]
        return value + pltpu.roll(value, rank, 1)

    e, c = jobs[-1]
    for d in order:
        r = pl.ds(pl.multiple_of(peer(d) * out_rows, out_rows), out_rows)
        lower(r, group(e), c)
        if d:
            for b in range(half_blocks):
                low_send[d - 1, b * BLOCK:(b + 1) * BLOCK, :] = jnp.where(
                    lane < rank, folded(d, b), folded(d, b + half_blocks)).astype(BF16)
            lcopy(d).start()
        else:
            for b in range(out_blocks):
                fold[b * BLOCK:(b + 1) * BLOCK, :] = folded(d, b)

    for e in range(1, groups):
        def one(j, carry, e=e):
            @pl.when(j != z)
            def _():
                uycopy(e, j, group(e)).wait_recv()
            return carry

        lax.fori_loop(0, owners, one, 0)

    def gather(step, carry):
        i, k = step // n_k, step % n_k
        r, c = tile_at(i, k)
        value = own[r, c]
        for d in range(1, tensors):
            xcopy(d, i, k).wait_recv()
            value = value + peer_part[d - 1, r, c].astype(F32)
        own[r, c] = value
        return carry

    lax.fori_loop(0, tiles, gather, 0)
    for d in range(1, tensors):
        lcopy(d).wait_recv()
    for b in range(half_blocks):
        at = pl.ds(b * BLOCK, BLOCK)
        first, second = fold[at, :], fold[pl.ds((b + half_blocks) * BLOCK, BLOCK), :]
        for d in range(1, tensors):
            got = low_recv[d - 1, at, :].astype(F32)
            other = pltpu.roll(got, rank, 1)
            first = first + jnp.where(lane < rank, got, other)
            second = second + jnp.where(lane < rank, other, got)
        for value, block in ((first, b), (second, b + half_blocks)):
            spread = jnp.concatenate([value] * (wide // LANES), axis=1)
            total[block * BLOCK:(block + 1) * BLOCK, :] = jnp.where(
                wide_lane == slot(0, block), spread, 0.0).astype(BF16)

    def finish(k, carry):
        c = pl.ds(pl.multiple_of(k * ct, ct), ct)
        value = own[:, c] + jnp.dot(
            total[...], up[:, :, c].reshape(wide, ct), preferred_element_type=F32)
        out_ref[:, c] = value.astype(BF16)
        return carry

    lax.fori_loop(0, n_k, finish, 0)

    for d in range(1, tensors):
        def left(step, carry, d=d):
            xcopy(d, step // n_k, step % n_k).wait_send()
            return carry

        lax.fori_loop(0, tiles, left, 0)
        lcopy(d).wait_send()

    def sent(j, carry):
        for step in (-1, 1):
            @pl.when(inside(z + step) & (step * (z - j) >= 0))
            def _():
                for c in range(CHUNKS):
                    zcopy(step, j, c).wait_send()
                ucopy(step, j).wait_send()

        @pl.when(j != z)
        def _():
            for e in range(1, groups):
                for c in range(CHUNKS):
                    ycopy(e, j, g, c).wait_send()
                uycopy(e, j, g).wait_send()
        return carry

    lax.fori_loop(0, owners, sent, 0)


def shards(mesh, tokens, weight, down, up, block_adapter, position):
    rows, feats = tokens.shape
    cols = weight.shape[1]
    rank = down.shape[2]
    owners, groups, tensors = (mesh.shape[a] for a in ("adapter", "groups", "tensor"))
    out_rows = rows // tensors
    mt, ct = min(256, out_rows), 256
    n_i, n_k = out_rows // mt, cols // ct
    wide = owners * rank
    peers, others = max(tensors - 1, 1), max(groups - 1, 1)
    dma = pltpu.SemaphoreType.DMA
    hbm = pl.BlockSpec(memory_space=pl.ANY)
    smem = pl.BlockSpec(memory_space=pltpu.SMEM)
    flops = 2 * rows * feats * (cols + wide) + 2 * out_rows * wide * cols
    return pl.pallas_call(
        functools.partial(kernel, (owners, groups, tensors, mt, ct)),
        out_shape=pltpu.VMEM((out_rows, cols), BF16),
        in_specs=[hbm, hbm, hbm, hbm, smem, smem],
        out_specs=pl.BlockSpec(memory_space=pltpu.VMEM),
        scratch_shapes=[
            pltpu.VMEM((rows, feats), BF16),
            pltpu.VMEM((feats, cols), BF16),
            pltpu.VMEM((owners, rank, feats), BF16),
            pltpu.VMEM((owners, rank, cols), BF16),
            pltpu.VMEM((peers, out_rows, cols), BF16),
            pltpu.VMEM((peers, out_rows, cols), BF16),
            pltpu.VMEM((out_rows, cols), F32),
            pltpu.VMEM((rows, wide), F32),
            pltpu.VMEM((out_rows, LANES), F32),
            pltpu.VMEM((peers, out_rows // 2, LANES), BF16),
            pltpu.VMEM((peers, out_rows // 2, LANES), BF16),
            pltpu.VMEM((out_rows, wide), BF16),
            dma((tensors, n_i)),
            dma((n_k,)),
            dma((2,)),
            dma((peers, n_i, n_k)),
            dma((peers, n_i, n_k)),
            dma((peers,)),
            dma((peers,)),
            dma((2, owners, CHUNKS)),
            dma((owners, CHUNKS)),
            dma((others, owners, CHUNKS)),
            dma((owners, groups, CHUNKS)),
            dma((2, owners)),
            dma((owners,)),
            dma((others, owners)),
            dma((owners, groups)),
        ],
        compiler_params=pltpu.CompilerParams(
            collective_id=0, has_side_effects=True, vmem_limit_bytes=56 * 2**20),
        cost_estimate=pl.CostEstimate(
            flops=flops, bytes_accessed=2 * (rows * feats + feats * cols), transcendentals=0),
    )(tokens, weight, down, up, block_adapter.reshape(-1), position)


def solution(mesh):
    placed = (
        P(("groups", "adapter"), "tensor"),
        P("tensor", "sub"),
        P("adapter", "sub", None, "tensor"),
        P("adapter", "sub", None, None),
        P("groups", None),
        P(),
    )
    return jax.shard_map(
        functools.partial(shards, mesh),
        mesh=mesh,
        in_specs=placed,
        out_specs=P(("groups", "adapter", "tensor"), "sub"),
        check_vma=False,
    )
```
